32 devices in a mesh: depth: 4 (over z), phi: 8 (over y, x, core).
Axes of the slice: x: 2, y: 2, z: 4, core: 2. Of those that a mesh axis runs over, the one named last changes fastest.
Arguments:
- grad_out: bfloat16 [448, 32, 32, 128], P('depth', 'phi'), may hold values from -6 to 6
- pre_act: bfloat16 [448, 32, 32, 128], P('depth', 'phi'), may hold values from -8 to 8
- w_first: bfloat16 [3, 3, 3, 32, 32], replicated, may hold values from -0.21875 to 0.21875
- w_second: bfloat16 [3, 3, 3, 32, 32], replicated, may hold values from -0.21875 to 0.21875
- map_blocks: bfloat16 [4096, 128, 128], P(('depth', 'phi')), may hold values from -0.15625 to 0.15625
- row_block: int32 [4096], P(('depth', 'phi')), may hold values from 0 to 447
- owner: int32 [4096, 1], P(('depth', 'phi')), may hold values from 0 to 31; in each aligned block of 128 rows (0 to 127, 128 to 255, ...) at most 8 rows name the same one
- col_local: int32 [4096], P(('depth', 'phi')), may hold values from 0 to 11
Outputs:
- cell_grad: float32 [384, 32, 128], P(('depth', 'phi'))
The draws below stay inside these ranges and needn't reach their ends.
Inputs may be any that keep to these rules, and one draw needn't show every extreme that they name: Among the 128 blocks of one device no owner is named more than 8 times, and in some devices one owner is named exactly 8 times; every owner is named by some block.
All inputs are finite; a program needn't handle non-finite values.
Results may differ from the reference program's by a relative error of at most 0.0033.
Values may be sent and summed in bfloat16 or wider, within the bound.
A program may use at most 192 MiB of HBM per device.

```python
import math
import jax
import jax.numpy as jnp
import numpy as np
from jax import lax

C = 32
E = 128
CBS = 128
PD = 4
DZ = 112
NB_DEV = 128
CB_DEV = 12
NZ = 448
NPHI = 32
OWNERS = 32
CAP = 8
BLOCKS = 4096
CELL_BLOCKS = 384
RB_DEV = 448
N_DEPTH = 4
N_PHI = 8


def touch_ends(array, own_key, smallest, top_value):
    place = [jax.random.randint(jax.random.fold_in(own_key, axis), (), 0, length) for axis, length in enumerate(array.shape)]
    main_axis = array.shape.index(max(array.shape))
    neighbour = place[:main_axis] + [(place[main_axis] + 1) % array.shape[main_axis]] + place[main_axis + 1:]
    return array.at[tuple(place)].set(smallest).at[tuple(neighbour)].set(top_value)


def steps_of(key, dims, shards, low, high):
    gain = 1.0
    for axis_at, blocks in shards:
        draws = jax.random.uniform(jax.random.fold_in(jax.random.fold_in(key, 6), axis_at), (blocks,), jnp.float32, low / len(shards), high / len(shards))
        gain = gain * jnp.repeat(jnp.exp(draws), dims[axis_at] // blocks).reshape((-1,) + (1,) * (len(dims) - 1 - axis_at))
    return gain


def routed_block(own_key, own, number, rows, number_of, top, limit, slope):
    ranking = jax.random.permutation(own_key, number_of)
    packed, usual = portions_of(number_of, rows * top, limit, slope, True), portions_of(number_of, rows * top, limit, slope, False)
    places = jnp.arange(number_of)

    def named(sizes, rotation):
        used = int((sizes > 0).sum())
        fixed = max(1, used // 4)
        passed = fixed + (places - fixed + rotation * (used - fixed)) % max(1, number_of - fixed)
        return jnp.zeros((number_of,), jnp.int32).at[ranking[jnp.where(places < fixed, places, passed)]].set(jnp.asarray(sizes, jnp.int32))

    sizes = jnp.where(number % 4 == 0, named(packed, number // 4), named(usual, number - number // 4 - 1))
    mixed = jax.random.permutation(jax.random.fold_in(own, 3), number_of)
    giver, taker = mixed[0:number_of // 2 * 2:2], mixed[1:number_of // 2 * 2:2]
    room = jnp.minimum(sizes[giver] - 1, limit - sizes[taker]) // 2
    room = jnp.where((giver == ranking[0]) | (taker == ranking[0]) | (sizes[taker] == 0), 0, jnp.maximum(room, 0))
    passed = jax.random.randint(jax.random.fold_in(own, 4), (number_of // 2,), 0, 1 << 20) % (room + 1)
    sizes = sizes.at[giver].add(-passed).at[taker].add(passed)
    items = jnp.searchsorted(jnp.cumsum(sizes), jnp.arange(rows * top), side="right").astype(jnp.int32)
    grid = items.reshape(top, rows).T
    grid = grid[jax.random.permutation(jax.random.fold_in(own, 1), rows)]
    rotation = jax.random.randint(jax.random.fold_in(own, 2), (rows, 1), 0, top)
    return jnp.take_along_axis(grid, (jnp.arange(top)[None, :] + rotation) % top, axis=1)


def portions_of(amount, total, reach, lean, full):
    loads = [(1 << 20) // math.isqrt(standing ** lean) + 1 for standing in range(1, amount + 1)]
    largest = reach if full else min(reach, max(-(-total // amount), total * loads[0] // sum(loads)))
    least = 1 if total - largest >= amount - 1 else 0
    given, surplus = [largest] + [least] * (amount - 1), total - largest - least * (amount - 1)
    while surplus > 0:
        candidates = [i for i in range(1, amount) if given[i] < largest] or [i for i in range(1, amount) if given[i] < reach]
        whole, left = sum([loads[i] for i in candidates]), surplus
        for i in candidates:
            more = min(reach - given[i], max(1, left * loads[i] // whole), surplus)
            given[i] = given[i] + more
            surplus = surplus - more
    return np.array(given)


def bell_draw(own_key, dims, deviation, most, split=(), dtype=jnp.bfloat16):
    values = deviation * jax.random.normal(own_key, dims, jnp.float32)
    if split:
        values = values * steps_of(own_key, dims, split, -0.22, 0.18)
    return jnp.clip(values, -most, most).astype(dtype)


def setup_inputs(seed: int = 0) -> dict:
    seeds = jax.random.split(jax.random.key(seed), 9)
    grad_out = bell_draw(seeds[0], (NZ, NPHI, C, E), 1.0, 6.0, ((0, 4), (1, 8)))
    pre_act = bell_draw(seeds[1], (NZ, NPHI, C, E), 1.5, 8.0, ((0, 4), (1, 8)))
    w_first = bell_draw(seeds[2], (3, 3, 3, C, C), (27 * C) ** -0.5, 0.21875)
    w_second = bell_draw(seeds[3], (3, 3, 3, C, C), (27 * C) ** -0.5, 0.21875)
    map_blocks = bell_draw(seeds[4], (BLOCKS, E, CBS), (E * NB_DEV // CB_DEV) ** -0.5, 0.15625, ((0, 32),))
    row_block = touch_ends(jax.random.randint(seeds[5], (BLOCKS,), 0, RB_DEV), jax.random.fold_in(seeds[5], 1), 0, RB_DEV - 1).astype(jnp.int32)
    owner_keys = jax.random.split(jax.random.fold_in(seeds[6], 1), BLOCKS // NB_DEV)
    owner_turns = jax.random.permutation(jax.random.fold_in(seeds[6], 3), BLOCKS // NB_DEV)
    owner = jax.vmap(lambda own, number: routed_block(jax.random.fold_in(seeds[6], 2), own, number, NB_DEV, OWNERS, 1, CAP, 2))(owner_keys, owner_turns).reshape((BLOCKS, 1))
    col_local = touch_ends(jax.random.randint(seeds[7], (BLOCKS,), 0, CB_DEV), jax.random.fold_in(seeds[7], 1), 0, CB_DEV - 1).astype(jnp.int32)
    return dict(grad_out=grad_out, pre_act=pre_act, w_first=w_first, w_second=w_second, map_blocks=map_blocks, row_block=row_block, owner=owner, col_local=col_local)


def adjoint_conv(field, weight):
    wrapped = jnp.concatenate([field[:, -1:], field, field[:, :1]], axis=1)
    lhs = jnp.transpose(wrapped, (2, 0, 1, 3))[None].astype(jnp.float32)
    kernel = jnp.transpose(jnp.flip(weight, (0, 1, 2)), (3, 4, 0, 1, 2)).astype(jnp.float32)
    result = lax.conv_general_dilated(lhs, kernel, (1, 1, 1), ((1, 1), (0, 0), (1, 1)), dimension_numbers=("NCDHW", "OIDHW", "NCDHW"), precision=lax.Precision.HIGHEST)
    return jnp.transpose(result[0], (1, 2, 0, 3))


def reference(grad_out, pre_act, w_first, w_second, map_blocks, row_block, owner, col_local):
    back_second = adjoint_conv(grad_out, w_second)
    pre_val = pre_act.astype(jnp.float32)
    sigmoid_p = jax.nn.sigmoid(pre_val)
    hidden_grad = (back_second * sigmoid_p * (1.0 + pre_val * (1.0 - sigmoid_p))).astype(jnp.bfloat16)
    grid_grad = (adjoint_conv(hidden_grad, w_first) + grad_out.astype(jnp.float32)).astype(jnp.bfloat16)
    devices_all = N_DEPTH * N_PHI
    per_device = grid_grad.reshape(N_DEPTH, DZ, N_PHI, PD, C, E).transpose(0, 2, 1, 3, 4, 5).reshape(devices_all, DZ * PD, C, E)
    block_vals = map_blocks.reshape(devices_all, NB_DEV, E, CBS)
    row_ids = row_block.reshape(devices_all, NB_DEV).astype(jnp.int32)
    target = (owner[:, 0] * CB_DEV + col_local).reshape(devices_all, NB_DEV).astype(jnp.int32)

    def visit(summed, inputs):
        grid_rows, values, row_index, cell_index = inputs
        picked = grid_rows[row_index].astype(jnp.float32)
        partial_value = jnp.einsum("nce,nek->nck", picked, values.astype(jnp.float32), precision=lax.Precision.HIGHEST)
        return summed.at[cell_index].add(partial_value), None

    start = jnp.zeros((CELL_BLOCKS, C, CBS), jnp.float32)
    summed, unused = lax.scan(visit, start, (per_device, block_vals, row_ids, target))
    return summed
```

```python
import jax
import jax.numpy as jnp
from jax import lax
from jax.experimental import pallas as pl
from jax.experimental.pallas import tpu as pltpu
from jax.sharding import PartitionSpec as P

CB_DEV = 12
VMEM_LIMIT = 48 * 1024 * 1024


def shift(block, axis, step, periodic):
    count = lax.axis_size(axis)
    pairs = [(i, i + step) for i in range(count) if 0 <= i + step < count]
    if periodic:
        pairs = [(i, (i + step) % count) for i in range(count)]
    return lax.ppermute(block, axis, pairs)


def edges_of(first_layer, last_layer):
    below = shift(last_layer, "depth", 1, False)
    above = shift(first_layer, "depth", -1, False)
    layers = jnp.stack([below, above])
    corner_low = shift(layers[:, -1], "phi", 1, True)
    corner_high = shift(layers[:, 0], "phi", -1, True)
    middle = layers.reshape(2, -1, layers.shape[-1])
    return jnp.concatenate([corner_low, middle, corner_high], axis=1)


def mixing(weight, phi_len):
    channels = weight.shape[3]
    base = jnp.transpose(weight[::-1, ::-1], (2, 3, 0, 1, 4))
    base = base.reshape(3, channels, 3, 3 * channels)
    rows = [
        jnp.pad(base, ((0, 0), (0, 0), (0, 0), (p * channels, (phi_len - 1 - p) * channels)))
        for p in range(phi_len)
    ]
    full = jnp.stack(rows, axis=1)
    return full.reshape(3 * phi_len * channels, 3 * (phi_len + 2) * channels)


def fill(xp, x_ref, low_ref, high_ref, edge_ref):
    depth = low_ref.shape[0]
    xp[0] = edge_ref[0]
    xp[depth + 1] = edge_ref[1]

    def step(z, carry):
        for k in range(4):
            d = z * 4 + k
            xp[d + 1, 0:32] = low_ref[d]
            xp[d + 1, 32:160] = x_ref[pl.ds(d * 4, 4)].reshape(128, 128)
            xp[d + 1, 160:192] = high_ref[d]
        return carry

    lax.fori_loop(0, depth // 4, step, 0)


def conv_pair(xp, w_ref, z):
    slabs = [xp[z + k] for k in range(4)]
    rhs = jnp.concatenate(
        [jnp.concatenate([slabs[k], slabs[k + 1]], axis=1) for k in range(3)], axis=0
    )
    y = jnp.dot(w_ref[...], rhs, preferred_element_type=jnp.float32)
    lane = lax.broadcasted_iota(jnp.int32, (128, 128), 1)
    outs = []
    for k in range(2):
        cols = slice(128 * k, 128 * k + 128)
        minus = pltpu.roll(y[0:128, cols], 127, 1)
        plus = pltpu.roll(y[256:384, cols], 1, 1)
        outs.append(
            y[128:256, cols]
            + jnp.where(lane == 127, 0.0, minus)
            + jnp.where(lane == 0, 0.0, plus)
        )
    return outs


def first_kernel(x_ref, low_ref, high_ref, edge_ref, pre_ref, w_ref, hid_ref, f0_ref, f3_ref, xp):
    fill(xp, x_ref, low_ref, high_ref, edge_ref)
    depth = low_ref.shape[0]

    def step(t, carry):
        z = t * 2
        for k, back in enumerate(conv_pair(xp, w_ref, z)):
            p = pre_ref[pl.ds((z + k) * 4, 4)].reshape(128, 128).astype(jnp.float32)
            s = 1.0 / (1.0 + jnp.exp(-p))
            hid = (back * s * (1.0 + p * (1.0 - s))).astype(jnp.bfloat16)
            hid_ref[pl.ds((z + k) * 4, 4)] = hid.reshape(4, 32, 128)
            f0_ref[z + k] = hid[0:32]
            f3_ref[z + k] = hid[96:128]
        return carry

    lax.fori_loop(0, depth // 2, step, 0)


def second_kernel(
    row_ref, pos_ref, x_ref, low_ref, high_ref, edge_ref, grad_ref, w_ref, map_ref, buf_ref, xp, grid
):
    fill(xp, x_ref, low_ref, high_ref, edge_ref)
    depth = low_ref.shape[0]

    def step(t, carry):
        z = t * 2
        for k, back in enumerate(conv_pair(xp, w_ref, z)):
            g = grad_ref[pl.ds((z + k) * 4, 4)].reshape(128, 128).astype(jnp.float32)
            grid[pl.ds((z + k) * 4, 4)] = (back + g).astype(jnp.bfloat16).reshape(4, 32, 128)
        return carry

    lax.fori_loop(0, depth // 2, step, 0)

    def clear(t, carry):
        buf_ref[pl.ds(t * 8, 8)] = jnp.zeros((8, 32, 128), jnp.bfloat16)
        return carry

    lax.fori_loop(0, buf_ref.shape[0] // 8, clear, 0)

    def block(t, carry):
        for k in range(4):
            n = t * 4 + k
            part = jnp.dot(grid[row_ref[n]], map_ref[n], preferred_element_type=jnp.float32)
            buf_ref[pos_ref[n]] = part.astype(jnp.bfloat16)
        return carry

    lax.fori_loop(0, map_ref.shape[0] // 4, block, 0)


def gather_kernel(target_ref, recv_ref, out_ref, acc):
    acc[...] = jnp.zeros_like(acc)

    def step(t, carry):
        for k in range(4):
            n = t * 4 + k
            c = target_ref[n]
            acc[c] = acc[c] + recv_ref[n].astype(jnp.float32)
        return carry

    lax.fori_loop(0, recv_ref.shape[0] // 4, step, 0)
    out_ref[...] = acc[0 : out_ref.shape[0]].astype(jnp.bfloat16)


def vmem():
    return pl.BlockSpec(memory_space=pltpu.VMEM)


def smem():
    return pl.BlockSpec(memory_space=pltpu.SMEM)


def body(grad_out, pre_act, w_first, w_second, map_blocks, row_block, owner, col_local):
    depth, phi_len, channels, eta = grad_out.shape
    rows = depth * phi_len
    bf16 = jnp.bfloat16
    depth_count = lax.axis_size("depth")
    phi_count = lax.axis_size("phi")
    owners = depth_count * phi_count
    block_count = map_blocks.shape[0]
    cell_size = map_blocks.shape[2]
    slots = max(2, 2 * block_count // owners)
    places = owners * slots
    padded = (depth + 2, (phi_len + 2) * channels, eta)

    low = shift(grad_out[:, -1], "phi", 1, True)
    high = shift(grad_out[:, 0], "phi", -1, True)
    edges = edges_of(grad_out[0], grad_out[-1])

    owner_ids = owner[:, 0]
    count = jnp.arange(block_count, dtype=jnp.int32)
    same = (owner_ids[:, None] == owner_ids[None, :]) & (count[None, :] < count[:, None])
    slot_index = jnp.sum(same.astype(jnp.int32), axis=1)
    owner_depth = owner_ids // phi_count
    owner_phi = owner_ids - owner_depth * phi_count
    position = (owner_phi * depth_count + owner_depth) * slots + slot_index
    taken = position[:, None] == jnp.arange(places, dtype=jnp.int32)[None, :]
    slot_cells = jnp.sum(
        jnp.where(taken, col_local.astype(jnp.float32)[:, None] + 1.0, 0.0), axis=0
    )
    got_cells = lax.all_to_all(
        slot_cells.reshape(phi_count, depth_count * slots), "phi", 0, 0, tiled=True
    )
    cells = got_cells.reshape(phi_count, depth_count, slots).astype(jnp.int32)
    base = (jnp.arange(depth_count, dtype=jnp.int32) * CB_DEV)[None, :, None]
    target = jnp.where(cells > 0, base + cells - 1, depth_count * CB_DEV).reshape(places)

    mix_second = mixing(w_second, phi_len)
    mix_first = mixing(w_first, phi_len)
    grad_rows = grad_out.reshape(rows, channels, eta)
    pre_rows = pre_act.reshape(rows, channels, eta)
    face = jax.ShapeDtypeStruct((depth, channels, eta), bf16)
    hidden, face_first, face_last = pl.pallas_call(
        first_kernel,
        out_shape=(jax.ShapeDtypeStruct((rows, channels, eta), bf16), face, face),
        in_specs=[vmem()] * 6,
        out_specs=(vmem(),) * 3,
        scratch_shapes=[pltpu.VMEM(padded, bf16)],
        compiler_params=pltpu.CompilerParams(vmem_limit_bytes=VMEM_LIMIT),
    )(grad_rows, low, high, edges, pre_rows, mix_second)

    hid_low = shift(face_last, "phi", 1, True)
    hid_high = shift(face_first, "phi", -1, True)
    hid_edges = edges_of(hidden[:phi_len], hidden[rows - phi_len :])
    buffer = pl.pallas_call(
        second_kernel,
        out_shape=jax.ShapeDtypeStruct((places, channels, cell_size), bf16),
        in_specs=[smem()] * 2 + [vmem()] * 7,
        out_specs=vmem(),
        scratch_shapes=[pltpu.VMEM(padded, bf16), pltpu.VMEM((rows, channels, eta), bf16)],
        compiler_params=pltpu.CompilerParams(vmem_limit_bytes=VMEM_LIMIT),
    )(row_block, position, hidden, hid_low, hid_high, hid_edges, grad_rows, mix_first, map_blocks)

    received = lax.all_to_all(
        buffer.reshape(phi_count, depth_count * slots, channels, cell_size), "phi", 0, 0, tiled=True
    ).reshape(places, channels, cell_size)
    sums = pl.pallas_call(
        gather_kernel,
        out_shape=jax.ShapeDtypeStruct((depth_count * CB_DEV, channels, cell_size), bf16),
        in_specs=[smem(), vmem()],
        out_specs=vmem(),
        scratch_shapes=[pltpu.VMEM((depth_count * CB_DEV + 1, channels, cell_size), jnp.float32)],
        compiler_params=pltpu.CompilerParams(vmem_limit_bytes=VMEM_LIMIT),
    )(target, received)
    parts = lax.all_to_all(
        sums.reshape(depth_count, CB_DEV, channels, cell_size), "depth", 0, 0, tiled=True
    )
    return jnp.sum(parts.astype(jnp.float32), axis=0)


def solution(mesh):
    return jax.shard_map(
        body,
        mesh=mesh,
        in_specs=(
            P("depth", "phi", None, None),
            P("depth", "phi", None, None),
            P(),
            P(),
            P(("depth", "phi"), None, None),
            P(("depth", "phi")),
            P(("depth", "phi"), None),
            P(("depth", "phi")),
        ),
        out_specs=P(("depth", "phi"), None, None),
        check_vma=False,
    )
```

```python
import jax
import jax.numpy as jnp
from jax import lax
from jax.experimental import pallas as pl
from jax.experimental.pallas import tpu as pltpu
from jax.sharding import PartitionSpec as P

CB_DEV = 12
VMEM_LIMIT = 48 * 1024 * 1024


def shift(block, axis, step, periodic):
    count = lax.axis_size(axis)
    pairs = [(i, i + step) for i in range(count) if 0 <= i + step < count]
    if periodic:
        pairs = [(i, (i + step) % count) for i in range(count)]
    return lax.ppermute(block, axis, pairs)


def edges_of(first_layer, last_layer):
    below = shift(last_layer, "depth", 1, False)
    above = shift(first_layer, "depth", -1, False)
    layers = jnp.stack([below, above])
    corner_low = shift(layers[:, -1], "phi", 1, True)
    corner_high = shift(layers[:, 0], "phi", -1, True)
    middle = layers.reshape(2, -1, layers.shape[-1])
    return jnp.concatenate([corner_low, middle, corner_high], axis=1)


def diagonal(block, depth_step, phi_step):
    depths, phis = lax.axis_size("depth"), lax.axis_size("phi")
    pairs = [
        (d * phis + p, (d + depth_step) * phis + (p + phi_step) % phis)
        for d in range(depths)
        for p in range(phis)
        if 0 <= d + depth_step < depths
    ]
    return lax.ppermute(block, ("depth", "phi"), pairs)


def direct_edges(first_layer, last_layer):
    sides = []
    for layer, step in ((last_layer, 1), (first_layer, -1)):
        low = diagonal(layer[-1], step, 1)
        high = diagonal(layer[0], step, -1)
        middle = shift(layer, "depth", step, False).reshape(-1, layer.shape[-1])
        sides.append(jnp.concatenate([low, middle, high]))
    return jnp.stack(sides)


def mixing(weight, phi_len):
    channels = weight.shape[3]
    base = jnp.transpose(weight[::-1, ::-1], (2, 3, 0, 1, 4))
    base = base.reshape(3, channels, 3, 3 * channels)
    rows = [
        jnp.pad(base, ((0, 0), (0, 0), (0, 0), (p * channels, (phi_len - 1 - p) * channels)))
        for p in range(phi_len)
    ]
    full = jnp.stack(rows, axis=1)
    return full.reshape(3 * phi_len * channels, 3 * (phi_len + 2) * channels)


def fill(xp, pieces):
    for x_ref, low_ref, high_ref, at, face_at, cells, to in pieces:

        def step(d, x_ref=x_ref, low_ref=low_ref, high_ref=high_ref, at=at, face_at=face_at, to=to):
            xp[to + d, 0:32] = low_ref[face_at + d]
            xp[to + d, 32:160] = x_ref[pl.ds((at + d) * 4, 4)].reshape(128, 128)
            xp[to + d, 160:192] = high_ref[face_at + d]

        whole = cells // 4 * 4
        if whole:

            def steps(t, carry, step=step):
                for k in range(4):
                    step(t * 4 + k)
                return carry

            lax.fori_loop(0, whole // 4, steps, 0)
        for d in range(whole, cells):
            step(d)


def conv_pair(xp, w_ref, z):
    slabs = [xp[z + k] for k in range(4)]
    rhs = jnp.concatenate(
        [jnp.concatenate([slabs[k], slabs[k + 1]], axis=1) for k in range(3)], axis=0
    )
    y = jnp.dot(w_ref[...], rhs, preferred_element_type=jnp.float32)
    lane = lax.broadcasted_iota(jnp.int32, (128, 128), 1)
    outs = []
    for k in range(2):
        cols = slice(128 * k, 128 * k + 128)
        minus = pltpu.roll(y[0:128, cols], 127, 1)
        plus = pltpu.roll(y[256:384, cols], 1, 1)
        outs.append(
            y[128:256, cols]
            + jnp.where(lane == 127, 0.0, minus)
            + jnp.where(lane == 0, 0.0, plus)
        )
    return outs


def convolve(xp, w_ref, cells, jump_at, jump_xp, depth_at, jump_depth, store):
    def step(t, carry):
        at = t * 2
        past = jnp.where(at >= jump_at, 1, 0)
        base = at + past * jump_xp
        z = at + depth_at + past * jump_depth
        for k, back in enumerate(conv_pair(xp, w_ref, base)):
            store(back, z + k, at + k)
        return carry

    lax.fori_loop(0, cells // 2, step, 0, unroll=4)


def store_hidden(pre_ref, hid_ref, f0_ref, f3_ref):
    def store(back, z, at):
        p = pre_ref[pl.ds(z * 4, 4)].reshape(128, 128).astype(jnp.float32)
        s = 1.0 / (1.0 + jnp.exp(-p))
        hid = (back * s * (1.0 + p * (1.0 - s))).astype(jnp.bfloat16)
        hid_ref[pl.ds(at * 4, 4)] = hid.reshape(4, 32, 128)
        f0_ref[at] = hid[0:32]
        f3_ref[at] = hid[96:128]

    return store


def first_middle(x, low, high, pre, w_ref, hid_ref, f0_ref, f3_ref, xp):
    depth = x.shape[0] // 4
    q = depth // 4
    fill(xp, [(x, low, high, q - 1, 0, depth - 2 * q + 2, 0)])
    m = depth - 2 * q
    convolve(xp, w_ref, m, m, 0, q, 0, store_hidden(pre, hid_ref, f0_ref, f3_ref))


def first_outer(after, x, low_m, high_m, low, high, edge, pre, w_ref, hid_ref, f0_ref, f3_ref, xp):
    depth = x.shape[0] // 4
    q = depth // 4
    m = depth - 2 * q + 2
    xp[0] = edge[0]
    xp[2 * q + 3] = edge[1]
    fill(
        xp,
        [
            (x, low, high, 0, 0, q - 1, 1),
            (x, low_m, high_m, q - 1, 0, 2, q),
            (x, low_m, high_m, depth - q - 1, m - 2, 2, q + 2),
            (x, low, high, depth - q + 1, q - 1, q - 1, q + 4),
        ],
    )
    store = store_hidden(pre, hid_ref, f0_ref, f3_ref)
    convolve(xp, w_ref, 2 * q, q, 2, 0, depth - 2 * q, store)


def second_middle(after, x, low, high, grad, w_ref, out_ref, xp):
    mid = x.shape[0] // 4
    q = mid // 2
    fill(xp, [(x, low, high, 3, 3, mid - 6, 0)])

    def store(back, z, at):
        g = grad[pl.ds(z * 4, 4)].reshape(128, 128).astype(jnp.float32)
        out_ref[pl.ds(at * 4, 4)] = (back + g).astype(jnp.bfloat16).reshape(4, 32, 128)

    convolve(xp, w_ref, mid - 8, mid, 0, q + 4, 0, store)


def second_outer(
    row_ref, pos_ref, x, low, high, x_m, low_m, high_m, edge, grad, mid_ref, w_ref, map_ref, buf_ref, xp, grid
):
    q = x.shape[0] // 8
    depth = grad.shape[0] // 4
    m = depth - 2 * q
    xp[0] = edge[0]
    xp[2 * q + 11] = edge[1]
    fill(
        xp,
        [
            (x, low, high, 0, 0, q, 1),
            (x_m, low_m, high_m, 0, 0, 5, q + 1),
            (x_m, low_m, high_m, m - 5, m - 5, 5, q + 6),
            (x, low, high, q, q, q, q + 11),
        ],
    )

    def store(back, z, at):
        g = grad[pl.ds(z * 4, 4)].reshape(128, 128).astype(jnp.float32)
        grid[pl.ds(z * 4, 4)] = (back + g).astype(jnp.bfloat16).reshape(4, 32, 128)

    convolve(xp, w_ref, 2 * q + 8, q + 4, 2, 0, depth - 2 * q - 8, store)

    def keep(t, carry):
        grid[pl.ds((q + 4) * 4 + t * 16, 16)] = mid_ref[pl.ds(t * 16, 16)]
        return carry

    lax.fori_loop(0, mid_ref.shape[0] // 16, keep, 0)

    def clear(t, carry):
        buf_ref[pl.ds(t * 8, 8)] = jnp.zeros((8, 32, 128), jnp.bfloat16)
        return carry

    lax.fori_loop(0, buf_ref.shape[0] // 8, clear, 0)

    def block(t, carry):
        for k in range(8):
            n = t * 8 + k
            part = jnp.dot(grid[row_ref[n]], map_ref[n], preferred_element_type=jnp.float32)
            buf_ref[pos_ref[n]] = part.astype(jnp.bfloat16)
        return carry

    lax.fori_loop(0, map_ref.shape[0] // 8, block, 0, unroll=2)


def gather_kernel(target_ref, recv_ref, out_ref, acc):
    acc[...] = jnp.zeros_like(acc)

    def step(t, carry):
        for k in range(4):
            n = t * 4 + k
            c = target_ref[n]
            acc[c] = acc[c] + recv_ref[n].astype(jnp.float32)
        return carry

    lax.fori_loop(0, recv_ref.shape[0] // 4, step, 0)
    out_ref[...] = acc[0 : out_ref.shape[0]].astype(jnp.bfloat16)


def vmem():
    return pl.BlockSpec(memory_space=pltpu.VMEM)


def smem():
    return pl.BlockSpec(memory_space=pltpu.SMEM)


def kernel(run, arrays, outs, scratch, cells, scalars=0, ordered=0):
    return pl.pallas_call(
        run,
        out_shape=outs,
        in_specs=[smem()] * scalars
        + [pl.BlockSpec(memory_space=pl.ANY)] * ordered
        + [vmem()] * arrays,
        out_specs=tuple(vmem() for _ in outs) if isinstance(outs, tuple) else vmem(),
        scratch_shapes=scratch,
        compiler_params=pltpu.CompilerParams(vmem_limit_bytes=VMEM_LIMIT),
        cost_estimate=pl.CostEstimate(
            flops=cells * 2 * 128 * 384 * 576, bytes_accessed=cells * 131072, transcendentals=0
        ),
    )


def body(grad_out, pre_act, w_first, w_second, map_blocks, row_block, owner, col_local):
    depth, phi_len, channels, eta = grad_out.shape
    rows = depth * phi_len
    bf16 = jnp.bfloat16
    depth_count = lax.axis_size("depth")
    phi_count = lax.axis_size("phi")
    owners = depth_count * phi_count
    block_count = map_blocks.shape[0]
    cell_size = map_blocks.shape[2]
    slots = max(2, 2 * block_count // owners)
    places = owners * slots
    q = depth // 4
    middle = depth - 2 * q

    def padded(cells):
        return pltpu.VMEM((cells, (phi_len + 2) * channels, eta), bf16)

    def outer_face(phi_at):
        return jnp.concatenate([grad_out[: q - 1, phi_at], grad_out[depth - q + 1 :, phi_at]])

    low_m = shift(grad_out[q - 1 : depth - q + 1, -1], "phi", 1, True)
    high_m = shift(grad_out[q - 1 : depth - q + 1, 0], "phi", -1, True)
    low_o = shift(outer_face(phi_len - 1), "phi", 1, True)
    high_o = shift(outer_face(0), "phi", -1, True)
    edges = edges_of(grad_out[0], grad_out[-1])

    owner_ids = owner[:, 0]
    count = jnp.arange(block_count, dtype=jnp.int32)
    same = (owner_ids[:, None] == owner_ids[None, :]) & (count[None, :] < count[:, None])
    slot_index = jnp.sum(same.astype(jnp.int32), axis=1)
    owner_depth = owner_ids // phi_count
    owner_phi = owner_ids - owner_depth * phi_count
    position = (owner_phi * depth_count + owner_depth) * slots + slot_index
    taken = position[:, None] == jnp.arange(places, dtype=jnp.int32)[None, :]
    slot_cells = jnp.sum(
        jnp.where(taken, col_local.astype(jnp.float32)[:, None] + 1.0, 0.0), axis=0
    )
    got_cells = lax.all_to_all(
        slot_cells.reshape(phi_count, depth_count * slots), "phi", 0, 0, tiled=True
    )
    cells = got_cells.reshape(phi_count, depth_count, slots).astype(jnp.int32)
    base = (jnp.arange(depth_count, dtype=jnp.int32) * CB_DEV)[None, :, None]
    target = jnp.where(cells > 0, base + cells - 1, depth_count * CB_DEV).reshape(places)

    mix_second = mixing(w_second, phi_len)
    mix_first = mixing(w_first, phi_len)
    grad_rows = grad_out.reshape(rows, channels, eta)
    pre_rows = pre_act.reshape(rows, channels, eta)
    def array(cells):
        return jax.ShapeDtypeStruct((cells, channels, eta), bf16)

    def hidden_outs(cells):
        return array(cells * phi_len), array(cells), array(cells)

    hid_m, hid_m0, hid_m3 = kernel(
        first_middle, 5, hidden_outs(middle), [padded(middle + 2)], middle
    )(grad_rows, low_m, high_m, pre_rows, mix_second)
    hid_low_m = shift(hid_m3, "phi", 1, True)
    hid_high_m = shift(hid_m0, "phi", -1, True)
    hid_o, hid_o0, hid_o3 = kernel(
        first_outer, 8, hidden_outs(2 * q), [padded(2 * q + 4)], 2 * q, ordered=1
    )(hid_m0, grad_rows, low_m, high_m, low_o, high_o, edges, pre_rows, mix_second)
    hid_low_o = shift(hid_o3, "phi", 1, True)
    hid_high_o = shift(hid_o0, "phi", -1, True)
    hid_edges = direct_edges(hid_o[:phi_len], hid_o[(2 * q - 1) * phi_len :])
    grid_m = kernel(
        second_middle, 5, array((middle - 8) * phi_len), [padded(middle - 6)], middle - 8, ordered=1
    )(hid_o0, hid_m, hid_low_m, hid_high_m, grad_rows, mix_first)
    buffer = kernel(
        second_outer,
        11,
        array(places),
        [padded(2 * q + 12), pltpu.VMEM((rows, channels, eta), bf16)],
        2 * q + 8,
        scalars=2,
    )(
        row_block, position, hid_o, hid_low_o, hid_high_o, hid_m, hid_low_m, hid_high_m,
        hid_edges, grad_rows, grid_m, mix_first, map_blocks,
    )

    received = lax.all_to_all(
        buffer.reshape(phi_count, depth_count * slots, channels, cell_size), "phi", 0, 0, tiled=True
    ).reshape(places, channels, cell_size)
    sums = pl.pallas_call(
        gather_kernel,
        out_shape=jax.ShapeDtypeStruct((depth_count * CB_DEV, channels, cell_size), bf16),
        in_specs=[smem(), vmem()],
        out_specs=vmem(),
        scratch_shapes=[pltpu.VMEM((depth_count * CB_DEV + 1, channels, cell_size), jnp.float32)],
        compiler_params=pltpu.CompilerParams(vmem_limit_bytes=VMEM_LIMIT),
    )(target, received)
    parts = lax.all_to_all(
        sums.reshape(depth_count, CB_DEV, channels, cell_size), "depth", 0, 0, tiled=True
    )
    return jnp.sum(parts.astype(jnp.float32), axis=0)


def solution(mesh):
    return jax.shard_map(
        body,
        mesh=mesh,
        in_specs=(
            P("depth", "phi", None, None),
            P("depth", "phi", None, None),
            P(),
            P(),
            P(("depth", "phi"), None, None),
            P(("depth", "phi")),
            P(("depth", "phi"), None),
            P(("depth", "phi")),
        ),
        out_specs=P(("depth", "phi"), None, None),
        check_vma=False,
    )
```

```python
import functools

import jax
import jax.numpy as jnp
from jax import lax
from jax.experimental import pallas as pl
from jax.experimental.pallas import tpu as pltpu
from jax.sharding import PartitionSpec as P

CB_DEV = 12
VMEM_LIMIT = 48 * 1024 * 1024


def mixing(weight, phi_len):
    channels = weight.shape[3]
    base = jnp.transpose(weight[::-1, ::-1], (2, 3, 0, 1, 4))
    base = base.reshape(3, channels, 3, 3 * channels)
    rows = [
        jnp.pad(base, ((0, 0), (0, 0), (0, 0), (p * channels, (phi_len - 1 - p) * channels)))
        for p in range(phi_len)
    ]
    full = jnp.stack(rows, axis=1)
    return full.reshape(3 * phi_len * channels, 3 * (phi_len + 2) * channels)


def conv_pair(xp, w_ref, z):
    slabs = [xp[z + k].reshape(192, 128) for k in range(4)]
    rhs = jnp.concatenate(
        [jnp.concatenate([slabs[k], slabs[k + 1]], axis=1) for k in range(3)], axis=0
    )
    y = jnp.dot(w_ref[...], rhs, preferred_element_type=jnp.float32)
    lane = lax.broadcasted_iota(jnp.int32, (128, 128), 1)
    outs = []
    for k in range(2):
        cols = slice(128 * k, 128 * k + 128)
        minus = pltpu.roll(y[0:128, cols], 127, 1)
        plus = pltpu.roll(y[256:384, cols], 1, 1)
        outs.append(
            y[128:256, cols]
            + jnp.where(lane == 127, 0.0, minus)
            + jnp.where(lane == 0, 0.0, plus)
        )
    return outs


def convolve(xp, w_ref, first, cells, store):
    def step(t, carry):
        z = first + t * 2
        for k, back in enumerate(conv_pair(xp, w_ref, z)):
            store(back, z + k)
        return carry

    lax.fori_loop(0, cells // 2, step, 0, unroll=4)


def grid_kernel(
    depths, phis, x_ref, pre_ref, w2_ref, w1_ref, out_ref, xp, hp, pre, send, recv, local
):
    depth = x_ref.shape[0]
    d = lax.axis_index("depth")
    p = lax.axis_index("phi")
    right = lax.rem(p + 1, phis)
    left = lax.rem(p + phis - 1, phis)
    inner = depth // 4 - 4
    core = depth // 4 + 4
    has_below = d > 0
    has_above = d < depths - 1
    mesh_ids = pl.DeviceIdType.MESH

    fill = pltpu.make_async_copy(x_ref, xp.at[pl.ds(1, depth), pl.ds(1, 4)], local.at[0])
    fill.start()
    load = pltpu.make_async_copy(pre_ref, pre, local.at[1])
    load.start()

    barrier = pltpu.get_barrier_semaphore()
    for q in (left, right):
        pl.semaphore_signal(barrier, inc=1, device_id=(d, q), device_id_type=mesh_ids)
    for exists, step in ((has_below, -1), (has_above, 1)):

        @pl.when(exists)
        def _(step=step):
            for q in (left, p, right):
                pl.semaphore_signal(barrier, inc=1, device_id=(d + step, q), device_id_type=mesh_ids)

    peers = 2 + 3 * has_below.astype(jnp.int32) + 3 * has_above.astype(jnp.int32)
    pl.semaphore_wait(barrier, peers)

    def remote(src, dst, stage, index, to):
        return pltpu.make_async_remote_copy(
            src_ref=src,
            dst_ref=dst,
            send_sem=send.at[stage, index],
            recv_sem=recv.at[stage, index],
            device_id=to,
            device_id_type=mesh_ids,
        )

    def faces(src, z_at, phi_at, dst, stage, index, first, cells):
        zs = pl.ds(first + z_at, cells)
        to = pl.ds(first + 1, cells)
        return [
            remote(src.at[zs, phi_at + 3], dst.at[to, 0], stage, index, (d, right)),
            remote(src.at[zs, phi_at], dst.at[to, 5], stage, index + 1, (d, left)),
        ]

    def layers(src, z_at, phi_at, dst, stage, step):
        z = z_at + (depth - 1 if step > 0 else 0)
        to = 0 if step > 0 else depth + 1
        index = 6 if step > 0 else 9
        mine = src.at[z]
        return [
            remote(mine.at[pl.ds(phi_at, 4)], dst.at[to, pl.ds(1, 4)], stage, index, (d + step, p)),
            remote(mine.at[phi_at + 3], dst.at[to, 0], stage, index + 1, (d + step, right)),
            remote(mine.at[phi_at], dst.at[to, 5], stage, index + 2, (d + step, left)),
        ]

    def sends(src, z_at, phi_at, dst, stage, cut):
        mid = faces(src, z_at, phi_at, dst, stage, 0, cut, depth - 2 * cut)
        outer = faces(src, z_at, phi_at, dst, stage, 2, 0, cut)
        outer += faces(src, z_at, phi_at, dst, stage, 4, depth - cut, cut)
        up = layers(src, z_at, phi_at, dst, stage, 1)
        down = layers(src, z_at, phi_at, dst, stage, -1)
        return mid, outer, up, down

    def start_outer(outer, up, down):
        for exists, group in ((has_above, up), (has_below, down)):

            @pl.when(exists)
            def _(group=group):
                for c in group:
                    c.start()

        for c in outer:
            c.start()

    def wait_outer(outer, up, down):
        for c in outer:
            c.wait_recv()
        for exists, group in ((has_below, up), (has_above, down)):

            @pl.when(exists)
            def _(group=group):
                for c in group:
                    c.wait_recv()

    first = sends(x_ref, 0, 0, xp, 0, inner - 1)
    second = sends(hp, 1, 1, hp, 1, inner)
    for c in first[0]:
        c.start()
    start_outer(*first[1:])

    zeros = jnp.zeros((6, 32, 128), jnp.bfloat16)
    for buf in (xp, hp):

        @pl.when(d == 0)
        def _(buf=buf):
            buf[0] = zeros

        @pl.when(d == depths - 1)
        def _(buf=buf):
            buf[depth + 1] = zeros

    def store_hidden(back, z):
        v = pre[z].reshape(128, 128).astype(jnp.float32)
        s = 1.0 / (1.0 + jnp.exp(-v))
        hid = (back * s * (1.0 + v * (1.0 - s))).astype(jnp.bfloat16)
        hp[z + 1, 1:5] = hid.reshape(4, 32, 128)

    def store_grid(back, z):
        g = xp[z + 1, 1:5].reshape(128, 128).astype(jnp.float32)
        out_ref[z] = (back + g).astype(jnp.bfloat16).reshape(4, 32, 128)

    fill.wait()
    load.wait()
    for c in first[0]:
        c.wait_recv()
    convolve(xp, w2_ref, inner, depth - 2 * inner, store_hidden)
    for c in second[0]:
        c.start()
    wait_outer(*first[1:])
    convolve(xp, w2_ref, 0, inner, store_hidden)
    convolve(xp, w2_ref, depth - inner, inner, store_hidden)
    start_outer(*second[1:])
    for c in second[0]:
        c.wait_recv()
    convolve(hp, w1_ref, core, depth - 2 * core, store_grid)
    wait_outer(*second[1:])
    convolve(hp, w1_ref, 0, core, store_grid)
    convolve(hp, w1_ref, depth - core, core, store_grid)
    for mid, outer, up, down in (first, second):
        for c in mid + outer:
            c.wait_send()
        for exists, group in ((has_above, up), (has_below, down)):

            @pl.when(exists)
            def _(group=group):
                for c in group:
                    c.wait_send()


def map_kernel(row_ref, pos_ref, grid, map_ref, buf_ref):
    def clear(t, carry):
        buf_ref[pl.ds(t * 8, 8)] = jnp.zeros((8, 32, 128), jnp.bfloat16)
        return carry

    lax.fori_loop(0, buf_ref.shape[0] // 8, clear, 0)

    def block(t, carry):
        for k in range(16):
            n = t * 16 + k
            part = jnp.dot(grid[row_ref[n]], map_ref[n], preferred_element_type=jnp.float32)
            buf_ref[pos_ref[n]] = part.astype(jnp.bfloat16)
        return carry

    lax.fori_loop(0, map_ref.shape[0] // 16, block, 0)


def gather_kernel(target_ref, recv_ref, out_ref, acc):
    acc[...] = jnp.zeros_like(acc)

    def step(t, carry):
        for k in range(4):
            n = t * 4 + k
            c = target_ref[n]
            acc[c] = acc[c] + recv_ref[n].astype(jnp.float32)
        return carry

    lax.fori_loop(0, recv_ref.shape[0] // 4, step, 0)
    out_ref[...] = acc[0 : out_ref.shape[0]].astype(jnp.bfloat16)


def vmem():
    return pl.BlockSpec(memory_space=pltpu.VMEM)


def smem():
    return pl.BlockSpec(memory_space=pltpu.SMEM)


def body(grad_out, pre_act, w_first, w_second, map_blocks, row_block, owner, col_local):
    depth, phi_len, channels, eta = grad_out.shape
    rows = depth * phi_len
    bf16 = jnp.bfloat16
    depth_count = lax.axis_size("depth")
    phi_count = lax.axis_size("phi")
    owners = depth_count * phi_count
    block_count = map_blocks.shape[0]
    cell_size = map_blocks.shape[2]
    slots = max(2, 2 * block_count // owners)
    places = owners * slots
    padded = (depth + 2, phi_len + 2, channels, eta)

    owner_ids = owner[:, 0]
    count = jnp.arange(block_count, dtype=jnp.int32)
    same = (owner_ids[:, None] == owner_ids[None, :]) & (count[None, :] < count[:, None])
    slot_index = jnp.sum(same.astype(jnp.int32), axis=1)
    owner_depth = owner_ids // phi_count
    owner_phi = owner_ids - owner_depth * phi_count
    position = (owner_phi * depth_count + owner_depth) * slots + slot_index
    taken = position[:, None] == jnp.arange(places, dtype=jnp.int32)[None, :]
    slot_cells = jnp.sum(
        jnp.where(taken, col_local.astype(jnp.float32)[:, None] + 1.0, 0.0), axis=0
    )
    got_cells = lax.all_to_all(
        slot_cells.reshape(phi_count, depth_count * slots), "phi", 0, 0, tiled=True
    )
    cells = got_cells.reshape(phi_count, depth_count, slots).astype(jnp.int32)
    base = (jnp.arange(depth_count, dtype=jnp.int32) * CB_DEV)[None, :, None]
    target = jnp.where(cells > 0, base + cells - 1, depth_count * CB_DEV).reshape(places)

    mix_second = mixing(w_second, phi_len)
    mix_first = mixing(w_first, phi_len)
    grid = pl.pallas_call(
        functools.partial(grid_kernel, depth_count, phi_count),
        out_shape=jax.ShapeDtypeStruct(grad_out.shape, bf16),
        in_specs=[pl.BlockSpec(memory_space=pl.ANY)] * 2 + [vmem()] * 2,
        out_specs=vmem(),
        scratch_shapes=[
            pltpu.VMEM(padded, bf16),
            pltpu.VMEM(padded, bf16),
            pltpu.VMEM(pre_act.shape[:1] + (phi_len, channels, eta), bf16),
            pltpu.SemaphoreType.DMA((2, 12)),
            pltpu.SemaphoreType.DMA((2, 12)),
            pltpu.SemaphoreType.DMA((2,)),
        ],
        compiler_params=pltpu.CompilerParams(
            vmem_limit_bytes=VMEM_LIMIT, collective_id=0, has_side_effects=True
        ),
    )(grad_out, pre_act, mix_second, mix_first)
    buffer = pl.pallas_call(
        map_kernel,
        out_shape=jax.ShapeDtypeStruct((places, channels, cell_size), bf16),
        in_specs=[smem()] * 2 + [vmem()] * 2,
        out_specs=vmem(),
        compiler_params=pltpu.CompilerParams(vmem_limit_bytes=VMEM_LIMIT),
    )(row_block, position, grid.reshape(rows, channels, eta), map_blocks)

    received = lax.all_to_all(
        buffer.reshape(phi_count, depth_count * slots, channels, cell_size), "phi", 0, 0, tiled=True
    ).reshape(places, channels, cell_size)
    sums = pl.pallas_call(
        gather_kernel,
        out_shape=jax.ShapeDtypeStruct((depth_count * CB_DEV, channels, cell_size), bf16),
        in_specs=[smem(), vmem()],
        out_specs=vmem(),
        scratch_shapes=[pltpu.VMEM((depth_count * CB_DEV + 1, channels, cell_size), jnp.float32)],
        compiler_params=pltpu.CompilerParams(vmem_limit_bytes=VMEM_LIMIT),
    )(target, received)
    parts = lax.all_to_all(
        sums.reshape(depth_count, CB_DEV, channels, cell_size), "depth", 0, 0, tiled=True
    )
    return jnp.sum(parts.astype(jnp.float32), axis=0)


def solution(mesh):
    return jax.shard_map(
        body,
        mesh=mesh,
        in_specs=(
            P("depth", "phi", None, None),
            P("depth", "phi", None, None),
            P(),
            P(),
            P(("depth", "phi"), None, None),
            P(("depth", "phi")),
            P(("depth", "phi"), None),
            P(("depth", "phi")),
        ),
        out_specs=P(("depth", "phi"), None, None),
        check_vma=False,
    )
```

```python
import functools

import jax
import jax.numpy as jnp
from jax import lax
from jax.experimental import pallas as pl
from jax.experimental.pallas import tpu as pltpu
from jax.sharding import PartitionSpec as P

CB_DEV = 12
VMEM_LIMIT = 48 * 1024 * 1024


def mixing(weight, phi_len):
    channels = weight.shape[3]
    base = jnp.transpose(weight[::-1, ::-1], (2, 3, 0, 1, 4))
    base = base.reshape(3, channels, 3, 3 * channels)
    rows = [
        jnp.pad(base, ((0, 0), (0, 0), (0, 0), (p * channels, (phi_len - 1 - p) * channels)))
        for p in range(phi_len)
    ]
    full = jnp.stack(rows, axis=1)
    return full.reshape(3 * phi_len * channels, 3 * (phi_len + 2) * channels)


def conv_pair(xp, w_ref, z):
    slabs = [xp[z + k].reshape(192, 128) for k in range(4)]
    rhs = jnp.concatenate(
        [jnp.concatenate([slabs[k], slabs[k + 1]], axis=1) for k in range(3)], axis=0
    )
    y = jnp.dot(w_ref[...], rhs, preferred_element_type=jnp.float32)
    lane = lax.broadcasted_iota(jnp.int32, (128, 128), 1)
    outs = []
    for k in range(2):
        cols = slice(128 * k, 128 * k + 128)
        minus = pltpu.roll(y[0:128, cols], 127, 1)
        plus = pltpu.roll(y[256:384, cols], 1, 1)
        outs.append(
            y[128:256, cols]
            + jnp.where(lane == 127, 0.0, minus)
            + jnp.where(lane == 0, 0.0, plus)
        )
    return outs


def convolve(xp, w_ref, first, cells, store):
    def step(t, carry):
        z = first + t * 2
        for k, back in enumerate(conv_pair(xp, w_ref, z)):
            store(back, z + k)
        return carry

    lax.fori_loop(0, cells // 2, step, 0, unroll=4)


def grid_kernel(
    depths, phis, x_ref, pre_ref, w2_ref, w1_ref, out_ref, xp, hp, pre, send, recv, local
):
    depth = x_ref.shape[0]
    d = lax.axis_index("depth")
    p = lax.axis_index("phi")
    right = lax.rem(p + 1, phis)
    left = lax.rem(p + phis - 1, phis)
    inner = depth // 4 - 4
    core = depth // 4 + 4
    has_below = d > 0
    has_above = d < depths - 1
    mesh_ids = pl.DeviceIdType.MESH

    fill = pltpu.make_async_copy(x_ref, xp.at[pl.ds(1, depth), pl.ds(1, 4)], local.at[0])
    fill.start()
    load = pltpu.make_async_copy(pre_ref, pre, local.at[1])
    load.start()

    barrier = pltpu.get_barrier_semaphore()
    for q in (left, right):
        pl.semaphore_signal(barrier, inc=1, device_id=(d, q), device_id_type=mesh_ids)
    for exists, step in ((has_below, -1), (has_above, 1)):

        @pl.when(exists)
        def _(step=step):
            for q in (left, p, right):
                pl.semaphore_signal(barrier, inc=1, device_id=(d + step, q), device_id_type=mesh_ids)

    peers = 2 + 3 * has_below.astype(jnp.int32) + 3 * has_above.astype(jnp.int32)
    pl.semaphore_wait(barrier, peers)

    def remote(src, dst, stage, index, to):
        return pltpu.make_async_remote_copy(
            src_ref=src,
            dst_ref=dst,
            send_sem=send.at[stage, index],
            recv_sem=recv.at[stage, index],
            device_id=to,
            device_id_type=mesh_ids,
        )

    def faces(src, z_at, phi_at, dst, stage, index, first, cells):
        zs = pl.ds(first + z_at, cells)
        to = pl.ds(first + 1, cells)
        return [
            remote(src.at[zs, phi_at + 3], dst.at[to, 0], stage, index, (d, right)),
            remote(src.at[zs, phi_at], dst.at[to, 5], stage, index + 1, (d, left)),
        ]

    def layers(src, z_at, phi_at, dst, stage, step):
        z = z_at + (depth - 1 if step > 0 else 0)
        to = 0 if step > 0 else depth + 1
        index = 6 if step > 0 else 9
        mine = src.at[z]
        return [
            remote(mine.at[pl.ds(phi_at, 4)], dst.at[to, pl.ds(1, 4)], stage, index, (d + step, p)),
            remote(mine.at[phi_at + 3], dst.at[to, 0], stage, index + 1, (d + step, right)),
            remote(mine.at[phi_at], dst.at[to, 5], stage, index + 2, (d + step, left)),
        ]

    def sends(src, z_at, phi_at, dst, stage, cut):
        mid = faces(src, z_at, phi_at, dst, stage, 0, cut, depth - 2 * cut)
        outer = faces(src, z_at, phi_at, dst, stage, 2, 0, cut)
        outer += faces(src, z_at, phi_at, dst, stage, 4, depth - cut, cut)
        up = layers(src, z_at, phi_at, dst, stage, 1)
        down = layers(src, z_at, phi_at, dst, stage, -1)
        return mid, outer, up, down

    def start_outer(outer, up, down):
        for exists, group in ((has_above, up), (has_below, down)):

            @pl.when(exists)
            def _(group=group):
                for c in group:
                    c.start()

        for c in outer:
            c.start()

    def wait_outer(outer, up, down):
        for c in outer:
            c.wait_recv()
        for exists, group in ((has_below, up), (has_above, down)):

            @pl.when(exists)
            def _(group=group):
                for c in group:
                    c.wait_recv()

    first = sends(x_ref, 0, 0, xp, 0, inner - 1)
    second = sends(hp, 1, 1, hp, 1, inner)
    for c in first[0]:
        c.start()
    start_outer(*first[1:])

    zeros = jnp.zeros((6, 32, 128), jnp.bfloat16)
    for buf in (xp, hp):

        @pl.when(d == 0)
        def _(buf=buf):
            buf[0] = zeros

        @pl.when(d == depths - 1)
        def _(buf=buf):
            buf[depth + 1] = zeros

    def store_hidden(back, z):
        v = pre[z].reshape(128, 128).astype(jnp.float32)
        s = 1.0 / (1.0 + jnp.exp(-v))
        hid = (back * s * (1.0 + v * (1.0 - s))).astype(jnp.bfloat16)
        hp[z + 1, 1:5] = hid.reshape(4, 32, 128)

    def store_grid(back, z):
        g = xp[z + 1, 1:5].reshape(128, 128).astype(jnp.float32)
        out_ref[z] = (back + g).astype(jnp.bfloat16).reshape(4, 32, 128)

    fill.wait()
    load.wait()
    for c in first[0]:
        c.wait_recv()
    convolve(xp, w2_ref, inner, depth - 2 * inner, store_hidden)
    for c in second[0]:
        c.start()
    wait_outer(*first[1:])
    convolve(xp, w2_ref, 0, inner, store_hidden)
    convolve(xp, w2_ref, depth - inner, inner, store_hidden)
    start_outer(*second[1:])
    for c in second[0]:
        c.wait_recv()
    convolve(hp, w1_ref, core, depth - 2 * core, store_grid)
    wait_outer(*second[1:])
    convolve(hp, w1_ref, 0, core, store_grid)
    convolve(hp, w1_ref, depth - core, core, store_grid)
    for mid, outer, up, down in (first, second):
        for c in mid + outer:
            c.wait_send()
        for exists, group in ((has_above, up), (has_below, down)):

            @pl.when(exists)
            def _(group=group):
                for c in group:
                    c.wait_send()


def map_kernel(row_ref, pos_ref, grid, map_ref, buf_ref):
    def clear(t, carry):
        buf_ref[pl.ds(t * 8, 8)] = jnp.zeros((8, 32, 128), jnp.bfloat16)
        return carry

    lax.fori_loop(0, buf_ref.shape[0] // 8, clear, 0)

    def block(t, carry):
        for k in range(16):
            n = t * 16 + k
            part = jnp.dot(grid[row_ref[n]], map_ref[n], preferred_element_type=jnp.float32)
            buf_ref[pos_ref[n]] = part.astype(jnp.bfloat16)
        return carry

    lax.fori_loop(0, map_ref.shape[0] // 16, block, 0)


def gather_kernel(target_ref, recv_ref, out_ref, acc):
    acc[...] = jnp.zeros_like(acc)

    def step(t, carry):
        for k in range(4):
            n = t * 4 + k
            c = target_ref[n]
            acc[c] = acc[c] + recv_ref[n].astype(jnp.float32)
        return carry

    lax.fori_loop(0, recv_ref.shape[0] // 4, step, 0)
    out_ref[...] = acc[0 : out_ref.shape[0]].astype(jnp.bfloat16)


def exchange_kernel(axis, count, x_ref, out_ref, send, recv, local):
    me = lax.axis_index(axis)
    barrier = pltpu.get_barrier_semaphore()
    peers = [lax.rem(me + k, count) for k in range(1, count)]
    for peer in peers:
        pl.semaphore_signal(
            barrier, inc=1, device_id={axis: peer}, device_id_type=pl.DeviceIdType.MESH
        )
    own = pltpu.make_async_copy(x_ref.at[me], out_ref.at[me], local)
    own.start()
    pl.semaphore_wait(barrier, count - 1)
    copies = [
        pltpu.make_async_remote_copy(
            src_ref=x_ref.at[peer],
            dst_ref=out_ref.at[me],
            send_sem=send.at[k],
            recv_sem=recv.at[k],
            device_id={axis: peer},
            device_id_type=pl.DeviceIdType.MESH,
        )
        for k, peer in enumerate(peers)
    ]
    for c in copies:
        c.start()
    own.wait()
    for c in copies:
        c.wait()


def exchange(x, axis, collective):
    count = lax.axis_size(axis)
    return pl.pallas_call(
        functools.partial(exchange_kernel, axis, count),
        out_shape=jax.ShapeDtypeStruct(x.shape, x.dtype),
        in_specs=[vmem()],
        out_specs=vmem(),
        scratch_shapes=[
            pltpu.SemaphoreType.DMA((count - 1,)),
            pltpu.SemaphoreType.DMA((count - 1,)),
            pltpu.SemaphoreType.DMA,
        ],
        compiler_params=pltpu.CompilerParams(
            vmem_limit_bytes=VMEM_LIMIT, collective_id=collective, has_side_effects=True
        ),
    )(x)


def vmem():
    return pl.BlockSpec(memory_space=pltpu.VMEM)


def smem():
    return pl.BlockSpec(memory_space=pltpu.SMEM)


def body(grad_out, pre_act, w_first, w_second, map_blocks, row_block, owner, col_local):
    depth, phi_len, channels, eta = grad_out.shape
    rows = depth * phi_len
    bf16 = jnp.bfloat16
    depth_count = lax.axis_size("depth")
    phi_count = lax.axis_size("phi")
    owners = depth_count * phi_count
    block_count = map_blocks.shape[0]
    cell_size = map_blocks.shape[2]
    slots = max(2, 2 * block_count // owners)
    places = owners * slots
    padded = (depth + 2, phi_len + 2, channels, eta)

    owner_ids = owner[:, 0]
    count = jnp.arange(block_count, dtype=jnp.int32)
    same = (owner_ids[:, None] == owner_ids[None, :]) & (count[None, :] < count[:, None])
    slot_index = jnp.sum(same.astype(jnp.int32), axis=1)
    owner_depth = owner_ids // phi_count
    owner_phi = owner_ids - owner_depth * phi_count
    position = (owner_phi * depth_count + owner_depth) * slots + slot_index
    taken = position[:, None] == jnp.arange(places, dtype=jnp.int32)[None, :]
    slot_cells = jnp.sum(
        jnp.where(taken, col_local.astype(jnp.float32)[:, None] + 1.0, 0.0), axis=0
    )
    got_cells = lax.all_to_all(
        slot_cells.reshape(phi_count, depth_count * slots), "phi", 0, 0, tiled=True
    )
    cells = got_cells.reshape(phi_count, depth_count, slots).astype(jnp.int32)
    base = (jnp.arange(depth_count, dtype=jnp.int32) * CB_DEV)[None, :, None]
    target = jnp.where(cells > 0, base + cells - 1, depth_count * CB_DEV).reshape(places)

    mix_second = mixing(w_second, phi_len)
    mix_first = mixing(w_first, phi_len)
    grid = pl.pallas_call(
        functools.partial(grid_kernel, depth_count, phi_count),
        out_shape=jax.ShapeDtypeStruct(grad_out.shape, bf16),
        in_specs=[pl.BlockSpec(memory_space=pl.ANY)] * 2 + [vmem()] * 2,
        out_specs=vmem(),
        scratch_shapes=[
            pltpu.VMEM(padded, bf16),
            pltpu.VMEM(padded, bf16),
            pltpu.VMEM(pre_act.shape[:1] + (phi_len, channels, eta), bf16),
            pltpu.SemaphoreType.DMA((2, 12)),
            pltpu.SemaphoreType.DMA((2, 12)),
            pltpu.SemaphoreType.DMA((2,)),
        ],
        compiler_params=pltpu.CompilerParams(
            vmem_limit_bytes=VMEM_LIMIT, collective_id=0, has_side_effects=True
        ),
    )(grad_out, pre_act, mix_second, mix_first)
    buffer = pl.pallas_call(
        map_kernel,
        out_shape=jax.ShapeDtypeStruct((places, channels, cell_size), bf16),
        in_specs=[smem()] * 2 + [vmem()] * 2,
        out_specs=vmem(),
        compiler_params=pltpu.CompilerParams(vmem_limit_bytes=VMEM_LIMIT),
    )(row_block, position, grid.reshape(rows, channels, eta), map_blocks)

    received = exchange(
        buffer.reshape(phi_count, depth_count * slots, channels, cell_size), "phi", 1
    ).reshape(places, channels, cell_size)
    sums = pl.pallas_call(
        gather_kernel,
        out_shape=jax.ShapeDtypeStruct((depth_count * CB_DEV, channels, cell_size), bf16),
        in_specs=[smem(), vmem()],
        out_specs=vmem(),
        scratch_shapes=[pltpu.VMEM((depth_count * CB_DEV + 1, channels, cell_size), jnp.float32)],
        compiler_params=pltpu.CompilerParams(vmem_limit_bytes=VMEM_LIMIT),
    )(target, received)
    parts = exchange(sums.reshape(depth_count, CB_DEV, channels, cell_size), "depth", 2)
    return jnp.sum(parts.astype(jnp.float32), axis=0)


def solution(mesh):
    return jax.shard_map(
        body,
        mesh=mesh,
        in_specs=(
            P("depth", "phi", None, None),
            P("depth", "phi", None, None),
            P(),
            P(),
            P(("depth", "phi"), None, None),
            P(("depth", "phi")),
            P(("depth", "phi"), None),
            P(("depth", "phi")),
        ),
        out_specs=P(("depth", "phi"), None, None),
        check_vma=False,
    )
```
